32 devices in a mesh: row: 16 (over z, y, core), proto: 2 (over x).
Axes of the slice: x: 2, y: 2, z: 4, core: 2. Of those that a mesh axis runs over, the one named last changes fastest.
Arguments:
- tokens: bfloat16 [8192, 4096], P('row'), may hold values from -6 to 6
- w_in: bfloat16 [4096, 8192], P('row', 'proto'), may hold values from -0.09375 to 0.09375
- w_out: bfloat16 [8192, 384], P('proto'), may hold values from -0.0625 to 0.0625
- teacher_z: bfloat16 [8192, 384], P(('row', 'proto')), may hold values from -6 to 6
- proto_student: bfloat16 [384, 49152], P(None, 'proto'), may hold values from -48 to 48
- proto_teacher: bfloat16 [384, 49152], P(None, 'proto'), may hold values from -48 to 48
- center: float32 [49152], P('proto'), may hold values from -0.6 to 0.6
- image_of: int32 [8192], P('row'), may hold values from 0 to 63
Outputs:
- loss: float32 [], replicated
- w_in_grad: float32 [4096, 8192], P('row', 'proto')
- w_out_grad: float32 [8192, 384], P('proto')
- proto_grad: float32 [384, 49152], P('row', 'proto')
The draws below stay inside these ranges and needn't reach their ends.
All inputs are finite; a program needn't handle non-finite values.
Results may differ from the reference program's by a relative error of at most 0.015.
Values may be sent and summed in bfloat16 or wider, within the bound.
No kernel may reach another device: no remote copies, remote signals or barrier semaphores. Data moves between devices by JAX's collectives and lax.ppermute only.
A program may use at most 256 MiB of HBM per device.

```python
import math
import jax
import jax.numpy as jnp
from jax import lax

D = 4096
H = 8192
B = 384
K = 49152
ROWS = 8192
IMAGES = 64


def column_spread(key):
    logs = jax.random.uniform(jax.random.fold_in(key, 21), (K,), jnp.float32, math.log(0.1), math.log(1.0))
    values = jax.random.normal(jax.random.fold_in(key, 23), (B, K), jnp.float32)
    return values * jnp.exp(logs)[None, :]


def draw_teacher_z(key, part):
    values = jnp.clip(jax.random.normal(jax.random.fold_in(key, 11), (ROWS, B), jnp.float32), -6.0, 6.0)
    return values.astype(jnp.bfloat16)


def draw_proto_teacher(key, part):
    values = column_spread(key)
    return jnp.clip(values, -48.0, 48.0).astype(jnp.bfloat16)


def draw_proto_student(key, part):
    values = column_spread(jax.random.fold_in(key, 31))
    return jnp.clip(values, -48.0, 48.0).astype(jnp.bfloat16)


def touch_ends(entries, stream_key, least, high):
    spot = [jax.random.randint(jax.random.fold_in(stream_key, axis), (), 0, length) for axis, length in enumerate(entries.shape)]
    widest = entries.shape.index(max(entries.shape))
    next_to = spot[:widest] + [(spot[widest] + 1) % entries.shape[widest]] + spot[widest + 1:]
    return entries.at[tuple(spot)].set(least).at[tuple(next_to)].set(high)


def level_of(stream_key, dims, pieces, least, largest):
    loudness = 1.0
    for position, shards_of in pieces:
        steps = jax.random.uniform(jax.random.fold_in(jax.random.fold_in(stream_key, 6), position), (shards_of,), jnp.float32, least / len(pieces), largest / len(pieces))
        loudness = loudness * jnp.repeat(jnp.exp(steps), dims[position] // shards_of).reshape((-1,) + (1,) * (len(dims) - 1 - position))
    return loudness


def centred(rng, dims, spread, reach, shards=(), kind=jnp.bfloat16):
    values = jax.random.normal(rng, dims, jnp.float32) * spread
    if len(shards) > 0:
        values = level_of(rng, dims, shards, -0.22, 0.18) * values
    return jnp.clip(values, min=-reach, max=reach).astype(kind)


def setup_inputs(seed: int = 0) -> dict:
    key_of = jax.random.split(jax.random.key(seed), 9)
    return {
        "tokens": centred(key_of[0], (ROWS, D), 1.0, 6.0, ((0, 16),)),
        "w_in": centred(key_of[1], (D, H), D ** -0.5, 0.09375, ((0, 16), (1, 2))),
        "w_out": centred(key_of[2], (H, B), H ** -0.5, 0.0625, ((0, 2),)),
        "teacher_z": draw_teacher_z(jax.random.fold_in(key_of[8], 71), 0),
        "proto_student": draw_proto_student(jax.random.fold_in(key_of[8], 71), 0),
        "proto_teacher": draw_proto_teacher(jax.random.fold_in(key_of[8], 71), 0),
        "center": centred(key_of[6], (K,), 0.1, 0.6, ((0, 2),), jnp.float32),
        "image_of": touch_ends(jax.random.randint(key_of[7], (ROWS,), 0, IMAGES), jax.random.fold_in(key_of[7], 1), 0, IMAGES - 1).astype(jnp.int32),
    }


tau_teacher = 0.07
tau_student = 0.1
loss_scale = 1048576.0
norm_eps = 1e-06

def gelu_parts(values):
    cumul = 0.5 * (1.0 + jax.scipy.special.erf(values * 0.7071067811865476))
    density = jnp.exp(-0.5 * values * values) * 0.3989422804014327
    return (values * cumul, cumul + values * density)

def inner(left, right):
    return lax.dot_general(left, right, (((0,), (0,)), ((), ())), preferred_element_type=jnp.float32)

def outer_last(left, right):
    return lax.dot_general(left, right, (((1,), (1,)), ((), ())), preferred_element_type=jnp.float32)

def reference(tokens, w_in, w_out, teacher_z, proto_student, proto_teacher, center, image_of):
    pre = jnp.dot(tokens, w_in, preferred_element_type=jnp.float32)
    act, slope = gelu_parts(pre)
    hidden = act.astype(jnp.bfloat16)
    bott = jnp.dot(hidden, w_out, preferred_element_type=jnp.float32)
    recip = lax.rsqrt(lax.optimization_barrier(jnp.sum(bott * bott, axis=1, keepdims=True)) + norm_eps)
    unit = bott * recip
    student_n = unit.astype(jnp.bfloat16)
    teach = teacher_z.astype(jnp.float32)
    teacher_n = (teach * lax.rsqrt(lax.optimization_barrier(jnp.sum(teach * teach, axis=1, keepdims=True)) + norm_eps)).astype(jnp.bfloat16)
    onehot = (image_of[:, None] == jnp.arange(IMAGES, dtype=jnp.int32)[None, :]).astype(jnp.float32)
    counts = lax.optimization_barrier(jnp.sum(onehot, axis=0))
    weight = 1.0 / (IMAGES * lax.optimization_barrier(jnp.sum(onehot * counts[None, :], axis=1)))
    block = 128
    blocks = ROWS // block

    def one_block(carry, index):
        grad_acc, loss_acc = carry
        begin = index * block
        s_rows = lax.dynamic_slice_in_dim(student_n, begin, block, 0)
        t_rows = lax.dynamic_slice_in_dim(teacher_n, begin, block, 0)
        w_rows = lax.dynamic_slice_in_dim(weight, begin, block, 0)
        logit_t = (jnp.dot(t_rows, proto_teacher, preferred_element_type=jnp.float32) - center[None, :]) / tau_teacher
        logit_s = jnp.dot(s_rows, proto_student, preferred_element_type=jnp.float32) / tau_student
        prob_t = jax.nn.softmax(logit_t, axis=1)
        logp_s = jax.nn.log_softmax(logit_s, axis=1)
        cross = -lax.optimization_barrier(jnp.sum(prob_t * logp_s, axis=1))
        grad_s = (loss_scale * w_rows[:, None] * (jnp.exp(logp_s) - prob_t) / tau_student).astype(jnp.bfloat16)
        grad_acc = grad_acc + inner(s_rows, grad_s)
        dnorm = outer_last(grad_s, proto_student)
        return ((grad_acc, loss_acc + jnp.sum(w_rows * cross)), dnorm)
    start_carry = (jnp.zeros((B, K), jnp.float32), jnp.zeros((), jnp.float32))
    (proto_grad, loss), dnorm = lax.scan(one_block, start_carry, jnp.arange(blocks, dtype=jnp.int32))
    dnorm = dnorm.reshape(ROWS, B)
    dbott = (recip * (dnorm - unit * lax.optimization_barrier(jnp.sum(unit * dnorm, axis=1, keepdims=True)))).astype(jnp.bfloat16)
    w_out_grad = inner(hidden, dbott)
    dpre = (outer_last(dbott, w_out) * slope).astype(jnp.bfloat16)
    w_in_grad = inner(tokens, dpre)
    return (loss, w_in_grad, w_out_grad, proto_grad)
```

```python
import functools
import math

import jax
import jax.numpy as jnp
from jax import lax
from jax.experimental import pallas as pl
from jax.experimental.pallas import tpu as pltpu
from jax.sharding import PartitionSpec as P

tau_teacher = 0.07
tau_student = 0.1
loss_scale = 1048576.0
norm_eps = 1e-06
log2e = 1.4426950408889634
bf16 = jnp.bfloat16
f32 = jnp.float32


def swap(value, bit, axis="row"):
    size = lax.axis_size(axis)
    return lax.ppermute(value, axis, [(i, i ^ bit) for i in range(size)])


def bits_of(size):
    return [1 << i for i in reversed(range(size.bit_length() - 1))]


def own_bit(axis, bit):
    return (lax.axis_index(axis) // bit) % 2


def halves(value, bit, axis, dim):
    half = value.shape[dim] // 2
    mine = own_bit(axis, bit)
    keep = lax.dynamic_slice_in_dim(value, mine * half, half, dim)
    send = lax.dynamic_slice_in_dim(value, (1 - mine) * half, half, dim)
    return keep, send


def in_order(own, other, bit, axis, dim):
    mine = own_bit(axis, bit)
    return jnp.where(
        mine == 0, jnp.concatenate([own, other], dim), jnp.concatenate([other, own], dim)
    )


def collect(value, axis, bits, dim):
    for bit in reversed(bits):
        value = in_order(value, swap(value, bit, axis), bit, axis, dim)
    return value


def tile_of(size, cap):
    best = 128
    for tile in range(128, cap + 1, 128):
        if size % tile == 0:
            best = tile
    return best


def log2_sum(first, second):
    top = jnp.maximum(first, second)
    return top + jnp.log2(jnp.exp2(first - top) + jnp.exp2(second - top))


def inner(left, right):
    return lax.dot_general(left, right, (((0,), (0,)), ((), ())), preferred_element_type=f32)


def outer_last(left, right):
    return lax.dot_general(left, right, (((1,), (1,)), ((), ())), preferred_element_type=f32)


def dot(left, right):
    return jnp.dot(left, right, preferred_element_type=f32)


def after(value, *others):
    return lax.optimization_barrier((value,) + others)[0] if others else value


def permute_body(order_ref, first_ref, second_ref, out_ref):
    rows, pair = first_ref.shape
    width = pair // 2
    flip = order_ref[0] % 2

    def place(low, high):
        for k, ref in enumerate((first_ref, second_ref)):
            at = pl.ds(k * rows, rows)
            out_ref[at, low : low + width] = ref[:, :width]
            out_ref[at, high : high + width] = ref[:, width:]

    @pl.when(flip == 0)
    def _():
        place(0, width)

    @pl.when(flip == 1)
    def _():
        place(width, 0)


def permute_columns(first, second, order):
    rows, columns = first.shape
    count = order.shape[0]
    width = 2 * columns // count
    block = pl.BlockSpec((rows, width), lambda j, order: (0, order[2 * j] // 2))
    return pl.pallas_call(
        permute_body,
        out_shape=jax.ShapeDtypeStruct((2 * rows, columns), first.dtype),
        grid_spec=pltpu.PrefetchScalarGridSpec(
            num_scalar_prefetch=1,
            grid=(count // 2,),
            in_specs=[block, block],
            out_specs=pl.BlockSpec((2 * rows, width), lambda j, order: (0, j)),
        ),
        compiler_params=pltpu.CompilerParams(vmem_limit_bytes=32 * 1024 * 1024),
        cost_estimate=pl.CostEstimate(
            flops=0, bytes_accessed=4 * rows * columns, transcendentals=0
        ),
        name="permute_columns",
    )(order, first, second)


def turn_body(in_ref, out_ref):
    out_ref[...] = in_ref[...].T


def turn_rows(value):
    rows, columns = value.shape
    wide = tile_of(columns, 512)
    return pl.pallas_call(
        turn_body,
        out_shape=jax.ShapeDtypeStruct((columns, rows), value.dtype),
        grid=(columns // wide,),
        in_specs=[pl.BlockSpec((rows, wide), lambda j: (0, j))],
        out_specs=pl.BlockSpec((wide, rows), lambda j: (j, 0)),
        compiler_params=pltpu.CompilerParams(vmem_limit_bytes=32 * 1024 * 1024),
        cost_estimate=pl.CostEstimate(
            flops=0, bytes_accessed=rows * columns, transcendentals=0
        ),
        name="turn_rows",
    )(value)


def grad_body(near_ref, far_ref, dnear_ref, dfar_ref, out_ref):
    total = dot(near_ref[...], dnear_ref[...]) + dot(far_ref[...], dfar_ref[...])
    out_ref[...] = total.astype(out_ref.dtype)


def grad_pass(near, far, dnear, dfar, piece, pieces):
    features, rows = near.shape
    wide = dnear.shape[1] // pieces
    high = tile_of(features, 512)
    block = pl.BlockSpec((high, rows), lambda i: (i, 0))
    strip = pl.BlockSpec((rows, wide), lambda i: (0, piece))
    return pl.pallas_call(
        grad_body,
        out_shape=jax.ShapeDtypeStruct((features, wide), bf16),
        grid=(features // high,),
        in_specs=[block, block, strip, strip],
        out_specs=pl.BlockSpec((high, wide), lambda i: (i, 0)),
        compiler_params=pltpu.CompilerParams(vmem_limit_bytes=32 * 1024 * 1024),
        cost_estimate=pl.CostEstimate(
            flops=features * rows * wide,
            bytes_accessed=2 * features * rows,
            transcendentals=0,
        ),
        name="grad_pass",
    )(near, far, dnear, dfar)


def softmax_body(scale, step, with_center, *refs):
    if with_center:
        _, n_ref, left_ref, center_ref, value_ref, e_ref, o_ref, lse_ref, logit = refs
    else:
        _, n_ref, left_ref, value_ref, e_ref, o_ref, lse_ref, logit = refs
    count = left_ref.shape[1]
    normed = n_ref[...]
    top = None
    for at in range(0, count, step):
        part = dot(normed, left_ref[:, at : at + step])
        if with_center:
            part = part - center_ref[:, at : at + step]
        logit[:, at : at + step] = part
        for k in range(0, step, 128):
            lanes = part[:, k : k + 128]
            top = lanes if top is None else jnp.maximum(top, lanes)
    top = jnp.max(top, axis=1, keepdims=True) * scale
    total, out = None, None
    for at in range(0, count, step):
        e = jnp.exp2(logit[:, at : at + step] * scale - top)
        for k in range(0, step, 128):
            lanes = e[:, k : k + 128]
            total = lanes if total is None else total + lanes
        low = e.astype(bf16)
        e_ref[:, at : at + step] = low
        product = outer_last(low, value_ref[:, at : at + step])
        out = product if out is None else out + product
    total = jnp.sum(total, axis=1, keepdims=True)
    o_ref[...] = out / total
    lane = lax.broadcasted_iota(jnp.int32, lse_ref.shape, 1)
    lse_ref[...] = jnp.where(lane == 0, top + jnp.log2(total), top)


def softmax_pass(normed, left, value, center, part, parts, tau):
    rows, width = normed.shape
    count = left.shape[1] // parts
    high = min(rows, 256)
    offset = part.astype(jnp.int32).reshape((1,))
    block = pl.BlockSpec((width, count), lambda i, off: (0, off[0]))
    by_row = lambda i, off: (i, 0)
    in_specs = [pl.BlockSpec((high, width), by_row), block]
    operands = [normed, left]
    if center is not None:
        in_specs.append(pl.BlockSpec((1, count), lambda i, off: (0, off[0])))
        operands.append(center.reshape((1, -1)))
    in_specs.append(block)
    operands.append(value)
    e, out, lse = pl.pallas_call(
        functools.partial(
            softmax_body, log2e / tau, tile_of(count, 1024), center is not None
        ),
        out_shape=(
            jax.ShapeDtypeStruct((rows, count), bf16),
            jax.ShapeDtypeStruct((rows, width), f32),
            jax.ShapeDtypeStruct((rows, 128), f32),
        ),
        grid_spec=pltpu.PrefetchScalarGridSpec(
            num_scalar_prefetch=1,
            grid=(rows // high,),
            in_specs=in_specs,
            out_specs=[
                pl.BlockSpec((high, count), by_row),
                pl.BlockSpec((high, width), by_row),
                pl.BlockSpec((high, 128), by_row),
            ],
            scratch_shapes=[pltpu.VMEM((high, count), f32)],
        ),
        compiler_params=pltpu.CompilerParams(vmem_limit_bytes=48 * 1024 * 1024),
        cost_estimate=pl.CostEstimate(
            flops=rows * width * count // 4,
            bytes_accessed=rows * count // 4,
            transcendentals=rows * count // 8,
        ),
        name="softmax_pass",
    )(offset, *operands)
    return e, out, lse[:, 0], lse[:, 1]


def head_body(rows_ref, early_ref, late_ref, w_ref, base_ref, hidden_ref, slope_ref, bott_ref):
    pre = early_ref[...] + dot(rows_ref[...], late_ref[...])
    size = jnp.abs(pre)
    gauss = jnp.exp2(pre * pre * (-0.5 * log2e))
    t = 1.0 / (1.0 + (0.3275911 * 0.7071067811865476) * size)
    poly = 1.061405429 * t - 1.453152027
    poly = poly * t + 1.421413741
    poly = poly * t - 0.284496736
    poly = poly * t + 0.254829592
    tail = (0.5 * poly) * t * gauss
    cumul = jnp.where(pre < 0.0, tail, 1.0 - tail)
    hidden = (pre * cumul).astype(bf16)
    hidden_ref[...] = hidden
    slope_ref[...] = (cumul + pre * gauss * 0.3989422804014327).astype(slope_ref.dtype)
    bott_ref[...] = base_ref[...] + dot(hidden, w_ref[...])


def head_pass(rows, early, late, w_out, base):
    count, wide = early.shape
    depth = late.shape[0]
    width = w_out.shape[1]
    last = rows.shape[1] // depth - 1
    high = min(count, 256)
    by_row = lambda i: (i, 0)
    whole = lambda i: (0, 0)
    return pl.pallas_call(
        head_body,
        out_shape=(
            jax.ShapeDtypeStruct((count, wide), bf16),
            jax.ShapeDtypeStruct((count, wide), bf16),
            jax.ShapeDtypeStruct((count, width), f32),
        ),
        grid=(count // high,),
        in_specs=[
            pl.BlockSpec((high, depth), lambda i: (i, last)),
            pl.BlockSpec((high, wide), by_row),
            pl.BlockSpec((depth, wide), whole),
            pl.BlockSpec((wide, width), whole),
            pl.BlockSpec((high, width), by_row),
        ],
        out_specs=[
            pl.BlockSpec((high, wide), by_row),
            pl.BlockSpec((high, wide), by_row),
            pl.BlockSpec((high, width), by_row),
        ],
        compiler_params=pltpu.CompilerParams(vmem_limit_bytes=32 * 1024 * 1024),
        cost_estimate=pl.CostEstimate(
            flops=2 * count * wide * (depth + width),
            bytes_accessed=8 * count * wide,
            transcendentals=2 * count * wide,
        ),
        name="head_pass",
    )(rows, early, late, w_out, base)


def proto_body(groups, n_ref, *refs):
    out_ref = refs[-1]
    total, at = None, 0
    for g in range(groups):
        es_ref, fs_ref, et_ref, ft_ref = refs[4 * g : 4 * g + 4]
        rows = es_ref.shape[0]
        grad = es_ref[...].astype(f32) * fs_ref[:, :1] - et_ref[...].astype(f32) * ft_ref[:, :1]
        product = dot(n_ref[:, at : at + rows], grad.astype(bf16))
        total = product if total is None else total + product
        at += rows
    out_ref[...] = total.astype(out_ref.dtype)


def proto_pass(turned, blocks, piece, pieces):
    width, rows = turned.shape
    count = blocks[0][0].shape[1]
    tile = tile_of(count // pieces, 512)
    tiles = count // pieces // tile
    first = piece * tiles
    whole = lambda j: (0, 0)
    strip = lambda j: (0, first + j)
    in_specs, operands = [pl.BlockSpec((width, rows), whole)], [turned]
    for block in blocks:
        for k, value in enumerate(block):
            if k % 2 == 0:
                in_specs.append(pl.BlockSpec((value.shape[0], tile), strip))
            else:
                in_specs.append(pl.BlockSpec(value.shape, whole))
            operands.append(value)
    return pl.pallas_call(
        functools.partial(proto_body, len(blocks)),
        out_shape=jax.ShapeDtypeStruct((width, count // pieces), bf16),
        grid=(tiles,),
        in_specs=in_specs,
        out_specs=pl.BlockSpec((width, tile), lambda j: (0, j)),
        compiler_params=pltpu.CompilerParams(vmem_limit_bytes=44 * 1024 * 1024),
        cost_estimate=pl.CostEstimate(
            flops=4 * rows * width * count // pieces,
            bytes_accessed=4 * rows * count // pieces,
            transcendentals=0,
        ),
        name="proto_pass",
    )(*operands)


def on_device(tokens, w_in, w_out, teacher_z, proto_student, proto_teacher, center, image_of):
    row_size = lax.axis_size("row")
    proto_size = lax.axis_size("proto")
    proto_bits = bits_of(proto_size)
    zhi, zlo, ybit, core = bits_of(row_size)
    row_index = lax.axis_index("row")
    proto_index = lax.axis_index("proto")
    part = own_bit("row", zlo) * 2 + own_bit("row", core)
    local = tokens.shape[0]
    features = tokens.shape[1]
    quarter = w_in.shape[1] // 4

    images = local * row_size // 128
    onehot = (image_of[:, None] == jnp.arange(images, dtype=jnp.int32)[None, :]).astype(f32)
    counts = jnp.sum(onehot, axis=0)
    for bit in (ybit, zhi, zlo, core):
        counts = counts + swap(counts, bit)

    def columns(index):
        return lax.dynamic_slice_in_dim(w_in, index * quarter, quarter, 1)

    chunks = 2 if quarter % 256 == 0 else 1
    chunk = quarter // chunks

    def cut(value, c):
        return lax.slice_in_dim(value, c * chunk, (c + 1) * chunk, axis=1)

    near, near_c = columns(part), columns(part ^ 1)
    far, far_c = columns(part ^ 2), columns(part ^ 3)
    from_core = after(swap(jnp.concatenate([near_c, far_c], 1), core), counts)
    mine = jnp.concatenate([near, from_core[:, :quarter]], 0)
    theirs = jnp.concatenate([far, from_core[:, quarter:]], 0)
    low = swap(theirs, zlo)
    own_h = [swap(cut(mine, 0), zhi)]
    for c in range(1, chunks):
        own_h.append(swap(after(cut(mine, c), own_h[-1]), zhi))
    own_y = swap(mine, ybit)

    strip = features // proto_size
    order = (jnp.arange(row_size, dtype=jnp.int32) ^ row_index).astype(jnp.int32)
    tokens_near = permute_columns(tokens, swap(tokens, core), order)

    def group_rows(value):
        value = collect(value, "proto", proto_bits, 0)
        far = swap(value, zlo)
        return [[value, swap(value, core)], [far, swap(far, core)]]

    def own_rows(value):
        for bit in proto_bits:
            value, _ = halves(value, bit, "proto", 0)
        return value

    def own_part(value, upto):
        for bit in proto_bits:
            if bit == upto:
                break
            value, _ = halves(value, bit, "proto", 0)
        return value

    def gather_passes(first, second, third):
        lse = jnp.stack([jnp.stack([first[2], third[2]]), second[2].reshape((2, local))])
        return [(p[0], p[3]) for p in (first, second, third)], (first[1], third[1]), lse

    def merge(near_out, far_out, lse):
        other = jnp.flip(swap(lse, zlo), 0)
        joint = log2_sum(lse, other)
        far_out = far_out.reshape((2, local, -1))
        out = [
            near_out[c] * jnp.exp2(lse[0, c] - joint[0, c])[:, None]
            + far_out[c].astype(f32) * jnp.exp2(other[0, c] - joint[0, c])[:, None]
            for c in (0, 1)
        ]
        lse = joint
        marks = [out[1]]
        got = swap(out[1].astype(bf16), core)
        other = jnp.flip(swap(lse, core), 1)
        joint = log2_sum(lse, other)
        out = (
            out[0] * jnp.exp2(lse[0, 0] - joint[0, 0])[:, None]
            + got.astype(f32) * jnp.exp2(other[0, 0] - joint[0, 0])[:, None]
        )
        lse = joint
        marks.append(out)
        own_lse = lse[0, 0]
        for bit in proto_bits:
            keep, given = halves(out, bit, "proto", 0)
            got = swap(given.astype(bf16), bit, "proto")
            other = swap(lse, bit, "proto")
            joint = log2_sum(lse, other)
            old, _ = halves(own_lse, bit, "proto", 0)
            new, _ = halves(own_part(joint[0, 0], bit), bit, "proto", 0)
            from_other, _ = halves(own_part(other[0, 0], bit), bit, "proto", 0)
            out = (
                keep * jnp.exp2(old - new)[:, None]
                + got.astype(f32) * jnp.exp2(from_other - new)[:, None]
            )
            lse = joint
            own_lse = new
        return out, own_lse, lse, marks

    teach = teacher_z.astype(f32)
    teacher_own = (
        teach * lax.rsqrt(jnp.sum(teach * teach, axis=1, keepdims=True) + norm_eps)
    ).astype(bf16)
    teacher_n = group_rows(teacher_own)
    run = functools.partial(
        softmax_pass,
        left=proto_teacher,
        value=proto_student,
        center=center,
        part=part,
        parts=4,
        tau=tau_teacher,
    )
    first = run(after(teacher_n[0][0], counts, tokens_near))
    low_y = swap(after(low, first[2]), ybit)
    third = run(after(teacher_n[0][1], first[2], own_y))
    piece = lax.dynamic_slice_in_dim(tokens, proto_index * strip, strip, 1)
    first_half = swap(after(piece[:, : strip // 2], low, third[2]), zlo)
    own_hy = [swap(value, ybit) for value in own_h]
    low_h = [swap(after(cut(low, 0), own_h[-1]), zhi)]
    second_half = swap(after(piece[:, strip // 2 :], first_half, own_h[-1]), zlo)
    turned_near = turn_rows(after(tokens_near, third[2]))
    second = run(after(jnp.concatenate(teacher_n[1], 0), third[2], *own_h, low_y, first_half, turned_near))
    far_t = swap(second[1].astype(bf16), zlo)
    low_h += [swap(after(cut(low, c), second[2]), zhi) for c in range(1, chunks)]
    low_hy = [swap(after(value, second[2]), ybit) for value in low_h]
    strips = [[first_half, second_half]]
    for bit in reversed(proto_bits):
        strips = strips + [[swap(value, bit, "proto") for value in pair] for pair in strips]
    tokens_far = jnp.concatenate([value for pair in strips for value in pair], 1)
    each = row_size // proto_size
    order_far = ((order // each) ^ proto_index) * each + order % each
    tokens_far = permute_columns(tokens_far, swap(tokens_far, core), order_far)
    et, near_t, lse_t = gather_passes(first, second, third)
    mean_t, _, lse_t, _ = merge(near_t, far_t, lse_t)

    weight = 1.0 / (images * jnp.sum(onehot * counts[None, :], axis=1))
    weight_far = swap(weight, zlo)
    pair = swap(jnp.stack([weight, weight_far]), core)
    weight = [[weight, pair[0]], [weight_far, pair[1]]]

    w_out_part = lax.dynamic_slice_in_dim(w_out, part * quarter, quarter, 0)
    slopes, hiddens = [[], []], [[], []]
    bott = [jnp.zeros((2 * local, w_out.shape[1]), f32)] * 2
    for c in range(chunks):
        early = [cut(value, c) for value in (mine, own_y, low, low_y)]
        early = jnp.concatenate(early + [own_h[c], own_hy[c]], 0)
        late = jnp.concatenate([low_h[c], low_hy[c]], 0)
        w_cut = w_out_part[c * chunk : (c + 1) * chunk]
        for z, rows in enumerate((tokens_near, tokens_far)):
            total = dot(rows[:, : early.shape[0]], early)
            hidden, slope, bott[z] = head_pass(rows, total, late, w_cut, bott[z])
            slopes[z].append(slope)
            hiddens[z].append(hidden)

    bott = [value[:local] + swap(value[local:], core) for value in bott]
    bott = bott[0] + swap(bott[1], zlo)
    for bit in proto_bits:
        keep, given = halves(bott, bit, "proto", 0)
        bott = keep + swap(given, bit, "proto")
    recip = lax.rsqrt(jnp.sum(bott * bott, axis=1, keepdims=True) + norm_eps)
    unit = bott * recip
    student_own = unit.astype(bf16)
    student_blocks = group_rows(student_own)
    run = functools.partial(
        softmax_pass,
        left=proto_student,
        value=proto_student,
        center=None,
        part=part,
        parts=4,
        tau=tau_student,
    )
    turned_far = turn_rows(tokens_far)
    first = run(after(student_blocks[0][0], turned_far))
    second = run(after(jnp.concatenate(student_blocks[1], 0), first[2]))
    far_s = swap(second[1].astype(bf16), zlo)
    third = run(after(student_blocks[0][1], second[2]))
    es, near_s, lse_s = gather_passes(first, second, third)
    mean_s, own_lse, lse_s, marks = merge(near_s, far_s, lse_s)

    weight_own = own_rows(weight[0][0])
    cross = own_lse / log2e - jnp.sum(student_own.astype(f32) * mean_t, axis=1) / tau_student
    loss = jnp.sum(weight_own * cross).reshape((1,))
    loss = loss + swap(loss, ybit)
    loss_y = loss
    loss = loss + swap(loss, zhi)

    coef = loss_scale / tau_student
    dnorm = (coef * weight_own)[:, None] * (mean_s - mean_t)
    dbott_own = (recip * (dnorm - unit * jnp.sum(unit * dnorm, axis=1, keepdims=True))).astype(bf16)
    dbott = group_rows(dbott_own)
    dbott = [jnp.concatenate(pair, 0) for pair in dbott]

    student_n = jnp.concatenate(
        [student_blocks[0][0], student_blocks[1][0], student_blocks[1][1], student_blocks[0][1]], 0
    )
    width = student_n.shape[1]
    share = width // row_size
    unit_index = jnp.arange(width, dtype=jnp.int32)
    source = ((unit_index // share) ^ row_index) * share + unit_index % share
    perm = (unit_index[:, None] == source[None, :]).astype(bf16)
    turned = lax.dot_general(
        perm, student_n, (((0,), (1,)), ((), ())), preferred_element_type=f32
    ).astype(bf16)

    def factors(passed, lse):
        out = []
        for (_, top), at in zip(passed, order_of):
            rows = jnp.concatenate([lse[z, c] for z, c in at])
            scale = jnp.concatenate([weight[z][c] for z, c in at])
            value = jnp.exp2(top - rows) * (coef * scale)
            out.append(jnp.broadcast_to(value[:, None], (value.shape[0], 128)))
        return out

    order_of = ([(0, 0)], [(1, 0), (1, 1)], [(0, 1)])
    scale_s = factors(es, lse_s)
    scale_t = factors(et, lse_t)
    count = es[0][0].shape[1]
    blocks = [(es[i][0], scale_s[i], et[i][0], scale_t[i]) for i in range(3)]

    def fold(value, ready=(), before=()):
        columns = value.shape[1]
        value = value.reshape((2, 2, 2, -1, columns))
        sent = swap(after(value[:, :, 1], *before), ybit)
        value = after(value[:, :, 0] + sent, *ready)
        value = value[0] + swap(value[1], zhi)
        value = value.reshape((2, 2, -1, columns))
        value = jnp.stack([value[:, 0], swap(value[:, 1], core)], 1)
        value = jnp.stack([value[0], swap(value[1], zlo)])
        return value.reshape((4, -1, columns)), sent

    def spread(pieces):
        whole = jnp.concatenate(pieces, 2)
        return jnp.concatenate(
            [lax.dynamic_index_in_dim(whole, part ^ q, 0, False) for q in range(4)], 1
        ).astype(f32)

    pieces = 2 if (count // 2) % 128 == 0 else 1
    proto_pieces, sent = [], []
    for i in range(pieces):
        value = proto_pass(after(turned, marks[i]), blocks, i, pieces)
        value, got = fold(value, tuple(dbott), (loss_y,))
        proto_pieces.append(value)
        sent.append(got)

    hidden = [jnp.concatenate(pair, 1) for pair in hiddens]
    w_out_grad = (inner(hidden[0], dbott[0]) + inner(hidden[1], dbott[1])).astype(bf16)
    product = w_out_grad
    loss = after(loss, product)
    for bit in (core, zlo):
        loss = loss + swap(loss, bit)
    for bit in proto_bits:
        loss = loss + swap(loss, bit, "proto")
    loss = loss[0]
    for bit in (ybit, zhi):
        keep, given = halves(w_out_grad, bit, "row", 0)
        w_out_grad = keep + swap(given, bit)
    for bit in (zhi, ybit):
        w_out_grad = in_order(w_out_grad, swap(w_out_grad, bit), bit, "row", 0)
    summed = w_out_grad
    w_out_grad = in_order(w_out_grad, swap(w_out_grad, zlo), zlo, "row", 0)
    w_out_grad = w_out_grad.reshape((2, 1, quarter, -1))
    w_out_grad = in_order(w_out_grad, swap(w_out_grad, core), core, "row", 1)
    w_out_grad = w_out_grad.reshape((4 * quarter, -1))

    w_in_pieces = []
    parts = 4 if quarter % 1024 == 0 else 2
    back = [
        outer_last(after(dbott[z], product), w_out_part)
        * jnp.concatenate(slopes[z], 1).astype(f32)
        for z in (0, 1)
    ]
    back = lax.optimization_barrier([value.astype(bf16) for value in back])
    grads = []
    for i in range(parts // 2):
        grad = grad_pass(turned_near, turned_far, *back, i, parts // 2)
        grads += jnp.split(grad, 2, axis=1)
    for i, grad in enumerate(grads):
        earlier = (sent[-2], summed) if i >= 2 else ()
        value, got = fold(grad, before=earlier)
        w_in_pieces.append(value)
        sent.append(got)
    return (loss, spread(w_in_pieces), w_out_grad.astype(f32), spread(proto_pieces))


def solution(mesh):
    return jax.shard_map(
        on_device,
        mesh=mesh,
        in_specs=(
            P("row", None),
            P("row", "proto"),
            P("proto", None),
            P(("row", "proto"), None),
            P(None, "proto"),
            P(None, "proto"),
            P("proto"),
            P("row"),
        ),
        out_specs=(P(), P("row", "proto"), P("proto", None), P("row", "proto")),
        check_vma=False,
    )
```

```python
import functools
import math

import jax
import jax.numpy as jnp
from jax import lax
from jax.experimental import pallas as pl
from jax.experimental.pallas import tpu as pltpu
from jax.sharding import PartitionSpec as P

tau_teacher = 0.07
tau_student = 0.1
loss_scale = 1048576.0
norm_eps = 1e-06
log2e = 1.4426950408889634
bf16 = jnp.bfloat16
f32 = jnp.float32


def swap(value, bit, axis="row"):
    size = lax.axis_size(axis)
    return lax.ppermute(value, axis, [(i, i ^ bit) for i in range(size)])


def bits_of(size):
    return [1 << i for i in reversed(range(size.bit_length() - 1))]


def own_bit(axis, bit):
    return (lax.axis_index(axis) // bit) % 2


def halves(value, bit, axis, dim):
    half = value.shape[dim] // 2
    mine = own_bit(axis, bit)
    keep = lax.dynamic_slice_in_dim(value, mine * half, half, dim)
    send = lax.dynamic_slice_in_dim(value, (1 - mine) * half, half, dim)
    return keep, send


def in_order(own, other, bit, axis, dim):
    mine = own_bit(axis, bit)
    return jnp.where(
        mine == 0, jnp.concatenate([own, other], dim), jnp.concatenate([other, own], dim)
    )


def collect(value, axis, bits, dim):
    for bit in reversed(bits):
        value = in_order(value, swap(value, bit, axis), bit, axis, dim)
    return value


def tile_of(size, cap):
    best = 128
    for tile in range(128, cap + 1, 128):
        if size % tile == 0:
            best = tile
    return best


def log2_sum(first, second):
    top = jnp.maximum(first, second)
    return top + jnp.log2(jnp.exp2(first - top) + jnp.exp2(second - top))


def inner(left, right):
    return lax.dot_general(left, right, (((0,), (0,)), ((), ())), preferred_element_type=f32)


def outer_last(left, right):
    return lax.dot_general(left, right, (((1,), (1,)), ((), ())), preferred_element_type=f32)


def dot(left, right):
    return jnp.dot(left, right, preferred_element_type=f32)


def after(value, *others):
    return lax.optimization_barrier((value,) + others)[0] if others else value


def together(*values):
    return lax.optimization_barrier(values)


def permute_body(order_ref, first_ref, second_ref, out_ref):
    rows, pair = first_ref.shape
    width = pair // 2
    flip = order_ref[0] % 2

    def place(low, high):
        for k, ref in enumerate((first_ref, second_ref)):
            at = pl.ds(k * rows, rows)
            out_ref[at, low : low + width] = ref[:, :width]
            out_ref[at, high : high + width] = ref[:, width:]

    @pl.when(flip == 0)
    def _():
        place(0, width)

    @pl.when(flip == 1)
    def _():
        place(width, 0)


def permute_columns(first, second, order):
    rows, columns = first.shape
    count = order.shape[0]
    width = 2 * columns // count
    block = pl.BlockSpec((rows, width), lambda j, order: (0, order[2 * j] // 2))
    return pl.pallas_call(
        permute_body,
        out_shape=jax.ShapeDtypeStruct((2 * rows, columns), first.dtype),
        grid_spec=pltpu.PrefetchScalarGridSpec(
            num_scalar_prefetch=1,
            grid=(count // 2,),
            in_specs=[block, block],
            out_specs=pl.BlockSpec((2 * rows, width), lambda j, order: (0, j)),
        ),
        compiler_params=pltpu.CompilerParams(vmem_limit_bytes=32 * 1024 * 1024),
        cost_estimate=pl.CostEstimate(
            flops=0, bytes_accessed=4 * rows * columns, transcendentals=0
        ),
        name="permute_columns",
    )(order, first, second)


def turn_body(in_ref, out_ref):
    out_ref[...] = in_ref[...].T


def turn_rows(value):
    rows, columns = value.shape
    wide = tile_of(columns, 512)
    return pl.pallas_call(
        turn_body,
        out_shape=jax.ShapeDtypeStruct((columns, rows), value.dtype),
        grid=(columns // wide,),
        in_specs=[pl.BlockSpec((rows, wide), lambda j: (0, j))],
        out_specs=pl.BlockSpec((wide, rows), lambda j: (j, 0)),
        compiler_params=pltpu.CompilerParams(vmem_limit_bytes=32 * 1024 * 1024),
        cost_estimate=pl.CostEstimate(
            flops=0, bytes_accessed=rows * columns, transcendentals=0
        ),
        name="turn_rows",
    )(value)


def grad_body(near_ref, far_ref, dnear_ref, dfar_ref, out_ref):
    total = dot(near_ref[...], dnear_ref[...]) + dot(far_ref[...], dfar_ref[...])
    out_ref[...] = total.astype(out_ref.dtype)


def grad_pass(near, far, dnear, dfar, piece, pieces):
    features, rows = near.shape
    wide = dnear.shape[1] // pieces
    high = tile_of(features, 512)
    block = pl.BlockSpec((high, rows), lambda i: (i, 0))
    strip = pl.BlockSpec((rows, wide), lambda i: (0, piece))
    return pl.pallas_call(
        grad_body,
        out_shape=jax.ShapeDtypeStruct((features, wide), bf16),
        grid=(features // high,),
        in_specs=[block, block, strip, strip],
        out_specs=pl.BlockSpec((high, wide), lambda i: (i, 0)),
        compiler_params=pltpu.CompilerParams(vmem_limit_bytes=32 * 1024 * 1024),
        cost_estimate=pl.CostEstimate(
            flops=8 * features * rows * wide,
            bytes_accessed=2 * features * rows,
            transcendentals=0,
        ),
        name="grad_pass",
    )(near, far, dnear, dfar)


def softmax_body(scale, step, with_center, *refs):
    if with_center:
        _, n_ref, left_ref, center_ref, value_ref, e_ref, o_ref, lse_ref, logit = refs
    else:
        _, n_ref, left_ref, value_ref, e_ref, o_ref, lse_ref, logit = refs
    count = left_ref.shape[1]
    normed = n_ref[...]
    top = None
    for at in range(0, count, step):
        part = dot(normed, left_ref[:, at : at + step])
        if with_center:
            part = part - center_ref[:, at : at + step]
        logit[:, at : at + step] = part
        for k in range(0, step, 128):
            lanes = part[:, k : k + 128]
            top = lanes if top is None else jnp.maximum(top, lanes)
    top = jnp.max(top, axis=1, keepdims=True) * scale
    total, out = None, None
    for at in range(0, count, step):
        e = jnp.exp2(logit[:, at : at + step] * scale - top)
        for k in range(0, step, 128):
            lanes = e[:, k : k + 128]
            total = lanes if total is None else total + lanes
        low = e.astype(bf16)
        e_ref[:, at : at + step] = low
        product = outer_last(low, value_ref[:, at : at + step])
        out = product if out is None else out + product
    total = jnp.sum(total, axis=1, keepdims=True)
    o_ref[...] = out / total
    lane = lax.broadcasted_iota(jnp.int32, lse_ref.shape, 1)
    lse_ref[...] = jnp.where(lane == 0, top + jnp.log2(total), top)


def softmax_pass(normed, left, value, center, part, parts, tau):
    rows, width = normed.shape
    count = left.shape[1] // parts
    high = min(rows, 256)
    offset = part.astype(jnp.int32).reshape((1,))
    block = pl.BlockSpec((width, count), lambda i, off: (0, off[0]))
    by_row = lambda i, off: (i, 0)
    in_specs = [pl.BlockSpec((high, width), by_row), block]
    operands = [normed, left]
    if center is not None:
        in_specs.append(pl.BlockSpec((1, count), lambda i, off: (0, off[0])))
        operands.append(center.reshape((1, -1)))
    in_specs.append(block)
    operands.append(value)
    e, out, lse = pl.pallas_call(
        functools.partial(
            softmax_body, log2e / tau, tile_of(count, 1024), center is not None
        ),
        out_shape=(
            jax.ShapeDtypeStruct((rows, count), bf16),
            jax.ShapeDtypeStruct((rows, width), f32),
            jax.ShapeDtypeStruct((rows, 128), f32),
        ),
        grid_spec=pltpu.PrefetchScalarGridSpec(
            num_scalar_prefetch=1,
            grid=(rows // high,),
            in_specs=in_specs,
            out_specs=[
                pl.BlockSpec((high, count), by_row),
                pl.BlockSpec((high, width), by_row),
                pl.BlockSpec((high, 128), by_row),
            ],
            scratch_shapes=[pltpu.VMEM((high, count), f32)],
        ),
        compiler_params=pltpu.CompilerParams(vmem_limit_bytes=48 * 1024 * 1024),
        cost_estimate=pl.CostEstimate(
            flops=rows * width * count * (24 if center is None else 1) // 4,
            bytes_accessed=rows * count * (8 if center is None else 1) // 4,
            transcendentals=rows * count // 8,
        ),
        name="softmax_pass",
    )(offset, *operands)
    return e, out, lse[:, 0], lse[:, 1]


def head_body(rows_ref, early_ref, late_ref, w_ref, base_ref, hidden_ref, slope_ref, bott_ref):
    pre = early_ref[...] + dot(rows_ref[...], late_ref[...])
    size = jnp.abs(pre)
    gauss = jnp.exp2(pre * pre * (-0.5 * log2e))
    t = 1.0 / (1.0 + (0.3275911 * 0.7071067811865476) * size)
    poly = 1.061405429 * t - 1.453152027
    poly = poly * t + 1.421413741
    poly = poly * t - 0.284496736
    poly = poly * t + 0.254829592
    tail = (0.5 * poly) * t * gauss
    cumul = jnp.where(pre < 0.0, tail, 1.0 - tail)
    hidden = (pre * cumul).astype(bf16)
    hidden_ref[...] = hidden
    slope_ref[...] = (cumul + pre * gauss * 0.3989422804014327).astype(slope_ref.dtype)
    bott_ref[...] = base_ref[...] + dot(hidden, w_ref[...])


def head_pass(rows, early, late, w_out, base):
    count, wide = early.shape
    depth = late.shape[0]
    width = w_out.shape[1]
    last = rows.shape[1] // depth - 1
    high = min(count, 256)
    by_row = lambda i: (i, 0)
    whole = lambda i: (0, 0)
    return pl.pallas_call(
        head_body,
        out_shape=(
            jax.ShapeDtypeStruct((count, wide), bf16),
            jax.ShapeDtypeStruct((count, wide), bf16),
            jax.ShapeDtypeStruct((count, width), f32),
        ),
        grid=(count // high,),
        in_specs=[
            pl.BlockSpec((high, depth), lambda i: (i, last)),
            pl.BlockSpec((high, wide), by_row),
            pl.BlockSpec((depth, wide), whole),
            pl.BlockSpec((wide, width), whole),
            pl.BlockSpec((high, width), by_row),
        ],
        out_specs=[
            pl.BlockSpec((high, wide), by_row),
            pl.BlockSpec((high, wide), by_row),
            pl.BlockSpec((high, width), by_row),
        ],
        compiler_params=pltpu.CompilerParams(vmem_limit_bytes=32 * 1024 * 1024),
        cost_estimate=pl.CostEstimate(
            flops=2 * count * wide * (depth + width),
            bytes_accessed=8 * count * wide,
            transcendentals=2 * count * wide,
        ),
        name="head_pass",
    )(rows, early, late, w_out, base)


def proto_body(groups, n_ref, *refs):
    out_ref = refs[-1]
    total, at = None, 0
    for g in range(groups):
        es_ref, fs_ref, et_ref, ft_ref = refs[4 * g : 4 * g + 4]
        rows = es_ref.shape[0]
        grad = es_ref[...].astype(f32) * fs_ref[:, :1] - et_ref[...].astype(f32) * ft_ref[:, :1]
        product = dot(n_ref[:, at : at + rows], grad.astype(bf16))
        total = product if total is None else total + product
        at += rows
    out_ref[...] = total.astype(out_ref.dtype)


def proto_pass(turned, blocks, piece, pieces):
    width, rows = turned.shape
    count = blocks[0][0].shape[1]
    tile = tile_of(count // pieces, 512)
    tiles = count // pieces // tile
    first = piece * tiles
    whole = lambda j: (0, 0)
    strip = lambda j: (0, first + j)
    in_specs, operands = [pl.BlockSpec((width, rows), whole)], [turned]
    for block in blocks:
        for k, value in enumerate(block):
            if k % 2 == 0:
                in_specs.append(pl.BlockSpec((value.shape[0], tile), strip))
            else:
                in_specs.append(pl.BlockSpec(value.shape, whole))
            operands.append(value)
    return pl.pallas_call(
        functools.partial(proto_body, len(blocks)),
        out_shape=jax.ShapeDtypeStruct((width, count // pieces), bf16),
        grid=(tiles,),
        in_specs=in_specs,
        out_specs=pl.BlockSpec((width, tile), lambda j: (0, j)),
        compiler_params=pltpu.CompilerParams(vmem_limit_bytes=44 * 1024 * 1024),
        cost_estimate=pl.CostEstimate(
            flops=4 * rows * width * count // pieces,
            bytes_accessed=4 * rows * count // pieces,
            transcendentals=0,
        ),
        name="proto_pass",
    )(*operands)


def on_device(tokens, w_in, w_out, teacher_z, proto_student, proto_teacher, center, image_of):
    row_size = lax.axis_size("row")
    proto_size = lax.axis_size("proto")
    proto_bits = bits_of(proto_size)
    zhi, zlo, ybit, core = bits_of(row_size)
    row_index = lax.axis_index("row")
    proto_index = lax.axis_index("proto")
    part = own_bit("row", zlo) * 2 + own_bit("row", core)
    local = tokens.shape[0]
    features = tokens.shape[1]
    quarter = w_in.shape[1] // 4

    images = local * row_size // 128
    onehot = (image_of[:, None] == jnp.arange(images, dtype=jnp.int32)[None, :]).astype(f32)
    counts = jnp.sum(onehot, axis=0)
    counts = counts + swap(counts, zlo)
    counts_zlo = counts
    for bit in (ybit, zhi, core):
        counts = counts + swap(counts, bit)

    def columns(index):
        return lax.dynamic_slice_in_dim(w_in, index * quarter, quarter, 1)

    chunks = 2 if quarter % 256 == 0 else 1
    chunk = quarter // chunks

    def cut(value, c):
        return lax.slice_in_dim(value, c * chunk, (c + 1) * chunk, axis=1)

    near, near_c = columns(part), columns(part ^ 1)
    far, far_c = columns(part ^ 2), columns(part ^ 3)
    from_core = after(swap(jnp.concatenate([near_c, far_c], 1), core), counts)
    mine = jnp.concatenate([near, from_core[:, :quarter]], 0)
    theirs = jnp.concatenate([far, from_core[:, quarter:]], 0)
    strip = features // proto_size
    order = (jnp.arange(row_size, dtype=jnp.int32) ^ row_index).astype(jnp.int32)
    tokens_core = swap(tokens, core)

    def group_rows(value):
        value = collect(value, "proto", proto_bits, 0)
        far = swap(value, zlo)
        return [[value, swap(value, core)], [far, swap(far, core)]]

    def own_rows(value):
        for bit in proto_bits:
            value, _ = halves(value, bit, "proto", 0)
        return value

    def own_part(value, upto):
        for bit in proto_bits:
            if bit == upto:
                break
            value, _ = halves(value, bit, "proto", 0)
        return value

    def gather_passes(first, second, third):
        lse = jnp.stack([jnp.stack([first[2], third[2]]), second[2].reshape((2, local))])
        return [(p[0], p[3]) for p in (first, second, third)], (first[1], third[1]), lse

    def merge(near_out, far_out, lse):
        other = jnp.flip(swap(lse, zlo), 0)
        joint = log2_sum(lse, other)
        far_out = far_out.reshape((2, local, -1))
        out = [
            near_out[c] * jnp.exp2(lse[0, c] - joint[0, c])[:, None]
            + far_out[c].astype(f32) * jnp.exp2(other[0, c] - joint[0, c])[:, None]
            for c in (0, 1)
        ]
        lse = joint
        marks = [out[1]]
        got = swap(out[1].astype(bf16), core)
        other = jnp.flip(swap(lse, core), 1)
        joint = log2_sum(lse, other)
        out = (
            out[0] * jnp.exp2(lse[0, 0] - joint[0, 0])[:, None]
            + got.astype(f32) * jnp.exp2(other[0, 0] - joint[0, 0])[:, None]
        )
        lse = joint
        marks.append(out)
        own_lse = lse[0, 0]
        for bit in proto_bits:
            keep, given = halves(out, bit, "proto", 0)
            got = swap(given.astype(bf16), bit, "proto")
            other = swap(lse, bit, "proto")
            joint = log2_sum(lse, other)
            old, _ = halves(own_lse, bit, "proto", 0)
            new, _ = halves(own_part(joint[0, 0], bit), bit, "proto", 0)
            from_other, _ = halves(own_part(other[0, 0], bit), bit, "proto", 0)
            out = (
                keep * jnp.exp2(old - new)[:, None]
                + got.astype(f32) * jnp.exp2(from_other - new)[:, None]
            )
            lse = joint
            own_lse = new
        return out, own_lse, lse, marks

    teach = teacher_z.astype(f32)
    teacher_own = (
        teach * lax.rsqrt(jnp.sum(teach * teach, axis=1, keepdims=True) + norm_eps)
    ).astype(bf16)
    teacher_near = collect(teacher_own, "proto", proto_bits, 0)
    teacher_core = swap(teacher_near, core)
    run = functools.partial(
        softmax_pass,
        left=proto_teacher,
        value=proto_student,
        center=center,
        part=part,
        parts=4,
        tau=tau_teacher,
    )
    piece = lax.dynamic_slice_in_dim(tokens, proto_index * strip, strip, 1)
    mine, theirs, teacher_near, teacher_core, tokens_core = together(
        mine, theirs, teacher_near, teacher_core, tokens_core
    )
    low = swap(theirs, zlo)
    own_y = swap(mine, ybit)
    own_h = [swap(cut(mine, 0), zhi)]
    teacher_far = swap(teacher_near, zlo)
    low, own_y, own_h[0], teacher_far = together(low, own_y, own_h[0], teacher_far)

    first = run(after(teacher_near, low))
    first_half = swap(after(piece[:, : strip // 2], low), zlo)
    low_y = swap(low, ybit)
    own_h += [swap(after(cut(mine, c), low), zhi) for c in range(1, chunks)]
    weight = 1.0 / (images * jnp.sum(onehot * counts[None, :], axis=1))
    weight_far = swap(weight, zlo)
    first_half, low_y, own_h[-1], weight_far, *first = together(
        first_half, low_y, own_h[-1], weight_far, *first
    )

    third = run(after(teacher_core, first_half))
    second_half = swap(after(piece[:, strip // 2 :], first_half), zlo)
    own_hy = swap(after(jnp.concatenate(own_h, 1), first_half), ybit)
    low_h = [swap(after(cut(low, 0), first_half), zhi)]
    strips = [[first_half]]
    for bit in reversed(proto_bits):
        strips = strips + [[swap(value, bit, "proto") for value in pair] for pair in strips]
    ends = [pair[0] for pair in strips[1:]]
    far_core = swap(teacher_far, core)
    second_half, own_hy, low_h[0], far_core, *rest = together(
        second_half, own_hy, low_h[0], far_core, *ends, *third
    )
    ends, third = rest[: len(ends)], rest[len(ends) :]
    strips = [[value] for value in [first_half] + ends]

    second = run(after(jnp.concatenate([teacher_far, far_core], 0), second_half))
    low_hy = [swap(after(low_h[0], second_half), ybit)]
    low_h += [swap(after(cut(low, c), second_half), zhi) for c in range(1, chunks)]
    ends = [second_half]
    for bit in reversed(proto_bits):
        ends = ends + [swap(value, bit, "proto") for value in ends]
    tokens_near = permute_columns(after(tokens, second_half), tokens_core, order)
    pair = swap(jnp.stack([weight, weight_far]), core)
    low_hy[0], low_h[-1], tokens_near, pair, *rest = together(
        low_hy[0], low_h[-1], tokens_near, pair, *ends, *second
    )
    weight = [[weight, pair[0]], [weight_far, pair[1]]]
    ends, second = rest[: len(ends)], rest[len(ends) :]
    strips = [pair + [value] for pair, value in zip(strips, ends)]
    low_hy += [swap(value, ybit) for value in low_h[1:]]
    far_t = swap(second[1].astype(bf16), zlo)
    tokens_far = jnp.concatenate([value for pair in strips for value in pair], 1)
    each = row_size // proto_size
    order_far = ((order // each) ^ proto_index) * each + order % each
    far_cores = swap(tokens_far, core)
    turned_near = turn_rows(tokens_near)
    tokens_far = permute_columns(tokens_far, far_cores, order_far)
    et, near_t, lse_t = gather_passes(first, second, third)
    mean_t, _, lse_t, _ = merge(near_t, far_t, lse_t)

    w_out_part = lax.dynamic_slice_in_dim(w_out, part * quarter, quarter, 0)
    slopes, hiddens = [[], []], [[], []]
    bott = [jnp.zeros((2 * local, w_out.shape[1]), f32)] * 2
    for c in range(chunks):
        early = [cut(value, c) for value in (mine, own_y, low, low_y)]
        early = jnp.concatenate(early + [own_h[c], cut(own_hy, c)], 0)
        late = jnp.concatenate([low_h[c], low_hy[c]], 0)
        w_cut = w_out_part[c * chunk : (c + 1) * chunk]
        for z, rows in enumerate((tokens_near, tokens_far)):
            total = dot(rows[:, : early.shape[0]], early)
            hidden, slope, bott[z] = head_pass(rows, total, late, w_cut, bott[z])
            slopes[z].append(slope)
            hiddens[z].append(hidden)

    bott = [value[:local] + swap(after(value[local:], mean_t, lse_t), core) for value in bott]
    bott, turned_near = together(bott[0] + swap(bott[1], zlo), turned_near)
    for bit in proto_bits:
        keep, given = halves(bott, bit, "proto", 0)
        bott = keep + swap(given, bit, "proto")
    bott, turned_far = together(bott, turn_rows(tokens_far))
    recip = lax.rsqrt(jnp.sum(bott * bott, axis=1, keepdims=True) + norm_eps)
    unit = bott * recip
    student_own = unit.astype(bf16)
    student_blocks = group_rows(student_own)
    run = functools.partial(
        softmax_pass,
        left=proto_student,
        value=proto_student,
        center=None,
        part=part,
        parts=4,
        tau=tau_student,
    )
    first = run(student_blocks[0][0])
    far_rows, *first = together(jnp.concatenate(student_blocks[1], 0), *first)
    second = run(far_rows)
    student_blocks[0][1], *second = together(student_blocks[0][1], *second)
    far_s = swap(second[1].astype(bf16), zlo)
    third = run(student_blocks[0][1])
    far_s, *third = together(far_s, *third)
    es, near_s, lse_s = gather_passes(first, second, third)
    mean_s, own_lse, lse_s, marks = merge(near_s, far_s, lse_s)

    weight_own = own_rows(weight[0][0])
    cross = own_lse / log2e - jnp.sum(student_own.astype(f32) * mean_t, axis=1) / tau_student
    loss = jnp.sum(weight_own * cross).reshape((1,))
    loss = loss + swap(loss, zhi)

    coef = loss_scale / tau_student
    dnorm = (coef * weight_own)[:, None] * (mean_s - mean_t)
    dbott_own = (recip * (dnorm - unit * jnp.sum(unit * dnorm, axis=1, keepdims=True))).astype(bf16)

    student_n = jnp.concatenate(
        [student_blocks[0][0], student_blocks[1][0], student_blocks[1][1], student_blocks[0][1]], 0
    )
    width = student_n.shape[1]
    share = width // row_size
    unit_index = jnp.arange(width, dtype=jnp.int32)
    source = ((unit_index // share) ^ row_index) * share + unit_index % share
    perm = (unit_index[:, None] == source[None, :]).astype(bf16)
    turned = lax.dot_general(
        perm, student_n, (((0,), (1,)), ((), ())), preferred_element_type=f32
    ).astype(bf16)

    def factors(passed, lse):
        out = []
        for (_, top), at in zip(passed, order_of):
            rows = jnp.concatenate([lse[z, c] for z, c in at])
            scale = jnp.concatenate([weight[z][c] for z, c in at])
            value = jnp.exp2(top - rows) * (coef * scale)
            out.append(jnp.broadcast_to(value[:, None], (value.shape[0], 128)))
        return out

    order_of = ([(0, 0)], [(1, 0), (1, 1)], [(0, 1)])
    scale_s = factors(es, lse_s)
    scale_t = factors(et, lse_t)
    count = es[0][0].shape[1]
    blocks = [(es[i][0], scale_s[i], et[i][0], scale_t[i]) for i in range(3)]

    def fold_y(value, *before):
        value = value.reshape((2, 2, 2, -1, value.shape[1]))
        sent = swap(after(value[:, :, 1], *before), ybit)
        return value[:, :, 0] + sent, sent

    def fold(value):
        columns = value.shape[-1]
        value = value[0] + swap(value[1], zhi)
        value = value.reshape((2, 2, -1, columns))
        value = jnp.stack([value[:, 0], swap(value[:, 1], core)], 1)
        value = jnp.stack([value[0], swap(value[1], zlo)])
        return value.reshape((4, -1, columns))

    def spread(pieces):
        whole = jnp.concatenate(pieces, 2)
        return jnp.concatenate(
            [lax.dynamic_index_in_dim(whole, part ^ q, 0, False) for q in range(4)], 1
        ).astype(f32)

    pieces = 2 if (count // 2) % 128 == 0 else 1
    proto_pieces, sent = [], []
    for i in range(pieces):
        value = proto_pass(after(turned, marks[i]), blocks, i, pieces)
        value, got = fold_y(value)
        proto_pieces.append(value)
        sent.append(got)
    dbott = collect(dbott_own, "proto", proto_bits, 0)
    dbott, loss, proto_pieces[0] = together(dbott, loss, proto_pieces[0])
    dbott_far = swap(dbott, zlo)
    dbott = [
        jnp.concatenate([dbott, swap(dbott, core)], 0),
        jnp.concatenate([dbott_far, swap(dbott_far, core)], 0),
    ]
    proto_pieces[0] = fold(proto_pieces[0])

    hidden = [jnp.concatenate(pair, 1) for pair in hiddens]
    w_out_grad = (inner(hidden[0], dbott[0]) + inner(hidden[1], dbott[1])).astype(bf16)
    product = w_out_grad
    parts = 2
    back = [
        outer_last(dbott[z], w_out_part) * jnp.concatenate(slopes[z], 1).astype(f32)
        for z in (0, 1)
    ]
    back = [value.astype(bf16) for value in back]
    *back, product, proto_pieces[-1] = together(*back, product, proto_pieces[-1])
    proto_pieces = proto_pieces[:1] + [fold(value) for value in proto_pieces[1:]]
    keep, given = halves(product, ybit, "row", 0)
    w_out_grad = keep + swap(given, ybit)
    sums = []
    for i in range(parts):
        grad = grad_pass(turned_near, turned_far, *back, i, parts)
        grad, back[0] = together(grad, back[0])
        sums += [fold_y(half)[0] for half in jnp.split(grad, 2, axis=1)]
    keep, given = halves(w_out_grad, zhi, "row", 0)
    w_out_grad = keep + swap(given, zhi)
    w_out_grad = in_order(w_out_grad, swap(w_out_grad, zhi), zhi, "row", 0)
    w_out_grad, loss, sums[0] = together(w_out_grad, loss, sums[0])
    for bit in proto_bits:
        loss = loss + swap(loss, bit, "proto")
    loss = loss + swap(loss, core)
    loss = loss + swap(loss, zlo)
    w_out_grad, loss, sums[-1] = together(w_out_grad, loss, sums[-1])
    w_out_grad = in_order(w_out_grad, swap(w_out_grad, ybit), ybit, "row", 0)
    w_out_grad = in_order(w_out_grad, swap(w_out_grad, zlo), zlo, "row", 0)
    w_in_pieces = [fold(value) for value in sums]
    w_out_grad = w_out_grad.reshape((2, 1, quarter, -1))
    w_out_grad = in_order(w_out_grad, swap(w_out_grad, core), core, "row", 1)
    w_out_grad = w_out_grad.reshape((4 * quarter, -1))
    loss = (loss + swap(loss, ybit))[0]
    return (loss, spread(w_in_pieces), w_out_grad.astype(f32), spread(proto_pieces))


def solution(mesh):
    return jax.shard_map(
        on_device,
        mesh=mesh,
        in_specs=(
            P("row", None),
            P("row", "proto"),
            P("proto", None),
            P(("row", "proto"), None),
            P(None, "proto"),
            P(None, "proto"),
            P("proto"),
            P("row"),
        ),
        out_specs=(P(), P("row", "proto"), P("proto", None), P("row", "proto")),
        check_vma=False,
    )
```

```python
import functools
import math

import jax
import jax.numpy as jnp
from jax import lax
from jax.experimental import pallas as pl
from jax.experimental.pallas import tpu as pltpu
from jax.sharding import PartitionSpec as P

tau_teacher = 0.07
tau_student = 0.1
loss_scale = 1048576.0
norm_eps = 1e-06
log2e = 1.4426950408889634
bf16 = jnp.bfloat16
f32 = jnp.float32


def swap(value, bit, axis="row"):
    size = lax.axis_size(axis)
    return lax.ppermute(value, axis, [(i, i ^ bit) for i in range(size)])


def bits_of(size):
    return [1 << i for i in reversed(range(size.bit_length() - 1))]


def own_bit(axis, bit):
    return (lax.axis_index(axis) // bit) % 2


def halves(value, bit, axis, dim):
    half = value.shape[dim] // 2
    mine = own_bit(axis, bit)
    keep = lax.dynamic_slice_in_dim(value, mine * half, half, dim)
    send = lax.dynamic_slice_in_dim(value, (1 - mine) * half, half, dim)
    return keep, send


def in_order(own, other, bit, axis, dim):
    mine = own_bit(axis, bit)
    return jnp.where(
        mine == 0, jnp.concatenate([own, other], dim), jnp.concatenate([other, own], dim)
    )


def collect(value, axis, bits, dim):
    for bit in reversed(bits):
        value = in_order(value, swap(value, bit, axis), bit, axis, dim)
    return value


def tile_of(size, cap):
    best = 128
    for tile in range(128, cap + 1, 128):
        if size % tile == 0:
            best = tile
    return best


def log2_sum(first, second):
    top = jnp.maximum(first, second)
    return top + jnp.log2(jnp.exp2(first - top) + jnp.exp2(second - top))


def inner(left, right):
    return lax.dot_general(left, right, (((0,), (0,)), ((), ())), preferred_element_type=f32)


def outer_last(left, right):
    return lax.dot_general(left, right, (((1,), (1,)), ((), ())), preferred_element_type=f32)


def dot(left, right):
    return jnp.dot(left, right, preferred_element_type=f32)


def after(value, *others):
    return lax.optimization_barrier((value,) + others)[0] if others else value


def together(*values):
    return lax.optimization_barrier(values)


def permute_body(order_ref, first_ref, second_ref, out_ref):
    rows, pair = first_ref.shape
    width = pair // 2
    flip = order_ref[0] % 2

    def place(low, high):
        for k, ref in enumerate((first_ref, second_ref)):
            at = pl.ds(k * rows, rows)
            out_ref[at, low : low + width] = ref[:, :width]
            out_ref[at, high : high + width] = ref[:, width:]

    @pl.when(flip == 0)
    def _():
        place(0, width)

    @pl.when(flip == 1)
    def _():
        place(width, 0)


def permute_columns(first, second, order):
    rows, columns = first.shape
    count = order.shape[0]
    width = 2 * columns // count
    block = pl.BlockSpec((rows, width), lambda j, order: (0, order[2 * j] // 2))
    return pl.pallas_call(
        permute_body,
        out_shape=jax.ShapeDtypeStruct((2 * rows, columns), first.dtype),
        grid_spec=pltpu.PrefetchScalarGridSpec(
            num_scalar_prefetch=1,
            grid=(count // 2,),
            in_specs=[block, block],
            out_specs=pl.BlockSpec((2 * rows, width), lambda j, order: (0, j)),
        ),
        compiler_params=pltpu.CompilerParams(vmem_limit_bytes=32 * 1024 * 1024),
        cost_estimate=pl.CostEstimate(
            flops=0, bytes_accessed=4 * rows * columns, transcendentals=0
        ),
        name="permute_columns",
    )(order, first, second)


def turn_body(in_ref, out_ref):
    out_ref[...] = in_ref[...].T


def turn_rows(value):
    rows, columns = value.shape
    wide = tile_of(columns, 512)
    return pl.pallas_call(
        turn_body,
        out_shape=jax.ShapeDtypeStruct((columns, rows), value.dtype),
        grid=(columns // wide,),
        in_specs=[pl.BlockSpec((rows, wide), lambda j: (0, j))],
        out_specs=pl.BlockSpec((wide, rows), lambda j: (j, 0)),
        compiler_params=pltpu.CompilerParams(vmem_limit_bytes=32 * 1024 * 1024),
        cost_estimate=pl.CostEstimate(
            flops=0, bytes_accessed=rows * columns, transcendentals=0
        ),
        name="turn_rows",
    )(value)


def grad_body(near_ref, far_ref, dnear_ref, dfar_ref, out_ref):
    total = dot(near_ref[...], dnear_ref[...]) + dot(far_ref[...], dfar_ref[...])
    out_ref[...] = total.astype(out_ref.dtype)


def grad_pass(near, far, dnear, dfar, piece, pieces):
    features, rows = near.shape
    wide = dnear.shape[1] // pieces
    high = tile_of(features, 512)
    block = pl.BlockSpec((high, rows), lambda i: (i, 0))
    strip = pl.BlockSpec((rows, wide), lambda i: (0, piece))
    return pl.pallas_call(
        grad_body,
        out_shape=jax.ShapeDtypeStruct((features, wide), bf16),
        grid=(features // high,),
        in_specs=[block, block, strip, strip],
        out_specs=pl.BlockSpec((high, wide), lambda i: (i, 0)),
        compiler_params=pltpu.CompilerParams(vmem_limit_bytes=32 * 1024 * 1024),
        cost_estimate=pl.CostEstimate(
            flops=8 * features * rows * wide,
            bytes_accessed=2 * features * rows,
            transcendentals=0,
        ),
        name="grad_pass",
    )(near, far, dnear, dfar)


def softmax_body(scale, step, with_center, *refs):
    if with_center:
        _, n_ref, left_ref, center_ref, value_ref, e_ref, o_ref, lse_ref, logit = refs
    else:
        _, n_ref, left_ref, value_ref, e_ref, o_ref, lse_ref, logit = refs
    count = left_ref.shape[1]
    normed = n_ref[...]
    top = None
    for at in range(0, count, step):
        part = dot(normed, left_ref[:, at : at + step])
        if with_center:
            part = part - center_ref[:, at : at + step]
        logit[:, at : at + step] = part
        for k in range(0, step, 128):
            lanes = part[:, k : k + 128]
            top = lanes if top is None else jnp.maximum(top, lanes)
    top = jnp.max(top, axis=1, keepdims=True) * scale
    total, out = None, None
    for at in range(0, count, step):
        e = jnp.exp2(logit[:, at : at + step] * scale - top)
        for k in range(0, step, 128):
            lanes = e[:, k : k + 128]
            total = lanes if total is None else total + lanes
        low = e.astype(bf16)
        e_ref[:, at : at + step] = low
        product = outer_last(low, value_ref[:, at : at + step])
        out = product if out is None else out + product
    total = jnp.sum(total, axis=1, keepdims=True)
    o_ref[...] = out / total
    lane = lax.broadcasted_iota(jnp.int32, lse_ref.shape, 1)
    lse_ref[...] = jnp.where(lane == 0, top + jnp.log2(total), top)


def softmax_pass(normed, left, value, center, part, parts, tau):
    rows, width = normed.shape
    count = left.shape[1] // parts
    high = min(rows, 256)
    offset = part.astype(jnp.int32).reshape((1,))
    block = pl.BlockSpec((width, count), lambda i, off: (0, off[0]))
    by_row = lambda i, off: (i, 0)
    in_specs = [pl.BlockSpec((high, width), by_row), block]
    operands = [normed, left]
    if center is not None:
        in_specs.append(pl.BlockSpec((1, count), lambda i, off: (0, off[0])))
        operands.append(center.reshape((1, -1)))
    in_specs.append(block)
    operands.append(value)
    e, out, lse = pl.pallas_call(
        functools.partial(
            softmax_body, log2e / tau, tile_of(count, 1024), center is not None
        ),
        out_shape=(
            jax.ShapeDtypeStruct((rows, count), bf16),
            jax.ShapeDtypeStruct((rows, width), f32),
            jax.ShapeDtypeStruct((rows, 128), f32),
        ),
        grid_spec=pltpu.PrefetchScalarGridSpec(
            num_scalar_prefetch=1,
            grid=(rows // high,),
            in_specs=in_specs,
            out_specs=[
                pl.BlockSpec((high, count), by_row),
                pl.BlockSpec((high, width), by_row),
                pl.BlockSpec((high, 128), by_row),
            ],
            scratch_shapes=[pltpu.VMEM((high, count), f32)],
        ),
        compiler_params=pltpu.CompilerParams(vmem_limit_bytes=48 * 1024 * 1024),
        cost_estimate=pl.CostEstimate(
            flops=rows * width * count * (24 if center is None else 1) // 4,
            bytes_accessed=rows * count * (8 if center is None else 1) // 4,
            transcendentals=rows * count // 8,
        ),
        name="softmax_pass",
    )(offset, *operands)
    return e, out, lse[:, 0], lse[:, 1]


def head_body(rows_ref, early_ref, late_ref, w_ref, base_ref, hidden_ref, slope_ref, bott_ref):
    pre = early_ref[...] + dot(rows_ref[...], late_ref[...])
    size = jnp.abs(pre)
    gauss = jnp.exp2(pre * pre * (-0.5 * log2e))
    t = 1.0 / (1.0 + (0.3275911 * 0.7071067811865476) * size)
    poly = 1.061405429 * t - 1.453152027
    poly = poly * t + 1.421413741
    poly = poly * t - 0.284496736
    poly = poly * t + 0.254829592
    tail = (0.5 * poly) * t * gauss
    cumul = jnp.where(pre < 0.0, tail, 1.0 - tail)
    hidden = (pre * cumul).astype(bf16)
    hidden_ref[...] = hidden
    slope_ref[...] = (cumul + pre * gauss * 0.3989422804014327).astype(slope_ref.dtype)
    bott_ref[...] = base_ref[...] + dot(hidden, w_ref[...])


def head_pass(rows, early, late, w_out, base):
    count, wide = early.shape
    depth = late.shape[0]
    width = w_out.shape[1]
    last = rows.shape[1] // depth - 1
    high = min(count, 256)
    by_row = lambda i: (i, 0)
    whole = lambda i: (0, 0)
    return pl.pallas_call(
        head_body,
        out_shape=(
            jax.ShapeDtypeStruct((count, wide), bf16),
            jax.ShapeDtypeStruct((count, wide), bf16),
            jax.ShapeDtypeStruct((count, width), f32),
        ),
        grid=(count // high,),
        in_specs=[
            pl.BlockSpec((high, depth), lambda i: (i, last)),
            pl.BlockSpec((high, wide), by_row),
            pl.BlockSpec((depth, wide), whole),
            pl.BlockSpec((wide, width), whole),
            pl.BlockSpec((high, width), by_row),
        ],
        out_specs=[
            pl.BlockSpec((high, wide), by_row),
            pl.BlockSpec((high, wide), by_row),
            pl.BlockSpec((high, width), by_row),
        ],
        compiler_params=pltpu.CompilerParams(vmem_limit_bytes=32 * 1024 * 1024),
        cost_estimate=pl.CostEstimate(
            flops=2 * count * wide * (depth + width),
            bytes_accessed=8 * count * wide,
            transcendentals=2 * count * wide,
        ),
        name="head_pass",
    )(rows, early, late, w_out, base)


def proto_body(groups, n_ref, *refs):
    out_ref = refs[-1]
    total, at = None, 0
    for g in range(groups):
        es_ref, fs_ref, et_ref, ft_ref = refs[4 * g : 4 * g + 4]
        rows = es_ref.shape[0]
        grad = es_ref[...].astype(f32) * fs_ref[:, :1] - et_ref[...].astype(f32) * ft_ref[:, :1]
        product = dot(n_ref[:, at : at + rows], grad.astype(bf16))
        total = product if total is None else total + product
        at += rows
    out_ref[...] = total.astype(out_ref.dtype)


def proto_pass(turned, blocks, piece, pieces):
    width, rows = turned.shape
    count = blocks[0][0].shape[1]
    tile = tile_of(count // pieces, 512)
    tiles = count // pieces // tile
    first = piece * tiles
    whole = lambda j: (0, 0)
    strip = lambda j: (0, first + j)
    in_specs, operands = [pl.BlockSpec((width, rows), whole)], [turned]
    for block in blocks:
        for k, value in enumerate(block):
            if k % 2 == 0:
                in_specs.append(pl.BlockSpec((value.shape[0], tile), strip))
            else:
                in_specs.append(pl.BlockSpec(value.shape, whole))
            operands.append(value)
    return pl.pallas_call(
        functools.partial(proto_body, len(blocks)),
        out_shape=jax.ShapeDtypeStruct((width, count // pieces), bf16),
        grid=(tiles,),
        in_specs=in_specs,
        out_specs=pl.BlockSpec((width, tile), lambda j: (0, j)),
        compiler_params=pltpu.CompilerParams(vmem_limit_bytes=44 * 1024 * 1024),
        cost_estimate=pl.CostEstimate(
            flops=4 * rows * width * count // pieces,
            bytes_accessed=4 * rows * count // pieces,
            transcendentals=0,
        ),
        name="proto_pass",
    )(*operands)


def on_device(tokens, w_in, w_out, teacher_z, proto_student, proto_teacher, center, image_of):
    row_size = lax.axis_size("row")
    proto_size = lax.axis_size("proto")
    proto_bits = bits_of(proto_size)
    zhi, zlo, ybit, core = bits_of(row_size)
    row_index = lax.axis_index("row")
    proto_index = lax.axis_index("proto")
    part = own_bit("row", zlo) * 2 + own_bit("row", core)
    local = tokens.shape[0]
    features = tokens.shape[1]
    quarter = w_in.shape[1] // 4

    images = local * row_size // 128
    onehot = (image_of[:, None] == jnp.arange(images, dtype=jnp.int32)[None, :]).astype(f32)
    counts = jnp.sum(onehot, axis=0)
    counts = counts + swap(counts, zlo)
    counts_zlo = counts
    for bit in (ybit, zhi, core):
        counts = counts + swap(counts, bit)

    def columns(index):
        return lax.dynamic_slice_in_dim(w_in, index * quarter, quarter, 1)

    chunks = 2 if quarter % 256 == 0 else 1
    chunk = quarter // chunks

    def cut(value, c):
        return lax.slice_in_dim(value, c * chunk, (c + 1) * chunk, axis=1)

    near, near_c = columns(part), columns(part ^ 1)
    far, far_c = columns(part ^ 2), columns(part ^ 3)
    from_core = after(swap(jnp.concatenate([near_c, far_c], 1), core), counts)
    mine = jnp.concatenate([near, from_core[:, :quarter]], 0)
    theirs = jnp.concatenate([far, from_core[:, quarter:]], 0)
    strip = features // proto_size
    order = (jnp.arange(row_size, dtype=jnp.int32) ^ row_index).astype(jnp.int32)
    tokens_core = swap(tokens, core)

    def group_rows(value):
        value = collect(value, "proto", proto_bits, 0)
        far = swap(value, zlo)
        return [[value, swap(value, core)], [far, swap(far, core)]]

    def own_rows(value):
        for bit in proto_bits:
            value, _ = halves(value, bit, "proto", 0)
        return value

    def own_part(value, upto):
        for bit in proto_bits:
            if bit == upto:
                break
            value, _ = halves(value, bit, "proto", 0)
        return value

    def gather_passes(first, second, third):
        lse = jnp.stack([jnp.stack([first[2], third[2]]), second[2].reshape((2, local))])
        return [(p[0], p[3]) for p in (first, second, third)], (first[1], third[1]), lse

    def merge(near_out, far_out, lse):
        other = jnp.flip(swap(lse, zlo), 0)
        joint = log2_sum(lse, other)
        far_out = far_out.reshape((2, local, -1))
        out = [
            near_out[c] * jnp.exp2(lse[0, c] - joint[0, c])[:, None]
            + far_out[c].astype(f32) * jnp.exp2(other[0, c] - joint[0, c])[:, None]
            for c in (0, 1)
        ]
        lse = joint
        marks = [out[1]]
        got = swap(out[1].astype(bf16), core)
        other = jnp.flip(swap(lse, core), 1)
        joint = log2_sum(lse, other)
        out = (
            out[0] * jnp.exp2(lse[0, 0] - joint[0, 0])[:, None]
            + got.astype(f32) * jnp.exp2(other[0, 0] - joint[0, 0])[:, None]
        )
        lse = joint
        marks.append(out)
        own_lse = lse[0, 0]
        for bit in proto_bits:
            keep, given = halves(out, bit, "proto", 0)
            got = swap(given.astype(bf16), bit, "proto")
            other = swap(lse, bit, "proto")
            joint = log2_sum(lse, other)
            old, _ = halves(own_lse, bit, "proto", 0)
            new, _ = halves(own_part(joint[0, 0], bit), bit, "proto", 0)
            from_other, _ = halves(own_part(other[0, 0], bit), bit, "proto", 0)
            out = (
                keep * jnp.exp2(old - new)[:, None]
                + got.astype(f32) * jnp.exp2(from_other - new)[:, None]
            )
            lse = joint
            own_lse = new
        return out, own_lse, lse, marks

    teach = teacher_z.astype(f32)
    teacher_own = (
        teach * lax.rsqrt(jnp.sum(teach * teach, axis=1, keepdims=True) + norm_eps)
    ).astype(bf16)
    teacher_near = collect(teacher_own, "proto", proto_bits, 0)
    teacher_core = swap(teacher_near, core)
    run = functools.partial(
        softmax_pass,
        left=proto_teacher,
        value=proto_student,
        center=center,
        part=part,
        parts=4,
        tau=tau_teacher,
    )
    piece = lax.dynamic_slice_in_dim(tokens, proto_index * strip, strip, 1)
    mine, theirs, teacher_near, teacher_core, tokens_core = together(
        mine, theirs, teacher_near, teacher_core, tokens_core
    )
    low = swap(theirs, zlo)
    own_y = swap(mine, ybit)
    own_h = [swap(cut(mine, 0), zhi)]
    teacher_far = swap(teacher_near, zlo)
    low, own_y, own_h[0], teacher_far = together(low, own_y, own_h[0], teacher_far)

    first = run(after(teacher_near, low))
    first_half = swap(after(piece[:, : strip // 2], low), zlo)
    low_y = swap(low, ybit)
    own_h += [swap(after(cut(mine, c), low), zhi) for c in range(1, chunks)]
    weight = 1.0 / (images * jnp.sum(onehot * counts[None, :], axis=1))
    weight_far = swap(weight, zlo)
    first_half, low_y, own_h[-1], weight_far, *first = together(
        first_half, low_y, own_h[-1], weight_far, *first
    )

    third = run(after(teacher_core, first_half))
    second_half = swap(after(piece[:, strip // 2 :], first_half), zlo)
    own_hy = swap(after(jnp.concatenate(own_h, 1), first_half), ybit)
    low_h = [swap(after(cut(low, 0), first_half), zhi)]
    strips = [[first_half]]
    for bit in reversed(proto_bits):
        strips = strips + [[swap(value, bit, "proto") for value in pair] for pair in strips]
    ends = [pair[0] for pair in strips[1:]]
    far_core = swap(teacher_far, core)
    second_half, own_hy, low_h[0], far_core, *rest = together(
        second_half, own_hy, low_h[0], far_core, *ends, *third
    )
    ends, third = rest[: len(ends)], rest[len(ends) :]
    strips = [[value] for value in [first_half] + ends]

    second = run(after(jnp.concatenate([teacher_far, far_core], 0), second_half))
    low_hy = [swap(after(low_h[0], second_half), ybit)]
    low_h += [swap(after(cut(low, c), second_half), zhi) for c in range(1, chunks)]
    ends = [second_half]
    for bit in reversed(proto_bits):
        ends = ends + [swap(value, bit, "proto") for value in ends]
    tokens_near = permute_columns(after(tokens, second_half), tokens_core, order)
    pair = swap(jnp.stack([weight, weight_far]), core)
    low_hy[0], low_h[-1], tokens_near, pair, *rest = together(
        low_hy[0], low_h[-1], tokens_near, pair, *ends, *second
    )
    weight = [[weight, pair[0]], [weight_far, pair[1]]]
    ends, second = rest[: len(ends)], rest[len(ends) :]
    strips = [pair + [value] for pair, value in zip(strips, ends)]
    low_hy += [swap(value, ybit) for value in low_h[1:]]
    far_t = swap(second[1].astype(bf16), zlo)
    tokens_far = jnp.concatenate([value for pair in strips for value in pair], 1)
    each = row_size // proto_size
    order_far = ((order // each) ^ proto_index) * each + order % each
    far_cores = swap(tokens_far, core)
    turned_near = turn_rows(tokens_near)
    tokens_far = permute_columns(tokens_far, far_cores, order_far)
    et, near_t, lse_t = gather_passes(first, second, third)
    mean_t, _, lse_t, _ = merge(near_t, far_t, lse_t)

    w_out_part = lax.dynamic_slice_in_dim(w_out, part * quarter, quarter, 0)
    slopes, hiddens = [[], []], [[], []]
    bott = [jnp.zeros((2 * local, w_out.shape[1]), f32)] * 2
    for c in range(chunks):
        early = [cut(value, c) for value in (mine, own_y, low, low_y)]
        early = jnp.concatenate(early + [own_h[c], cut(own_hy, c)], 0)
        late = jnp.concatenate([low_h[c], low_hy[c]], 0)
        w_cut = w_out_part[c * chunk : (c + 1) * chunk]
        for z, rows in enumerate((tokens_near, tokens_far)):
            total = dot(rows[:, : early.shape[0]], early)
            hidden, slope, bott[z] = head_pass(rows, total, late, w_cut, bott[z])
            slopes[z].append(slope)
            hiddens[z].append(hidden)

    bott = [value[:local] + swap(after(value[local:], mean_t, lse_t), core) for value in bott]
    bott, turned_near = together(bott[0] + swap(bott[1], zlo), turned_near)
    for bit in proto_bits:
        keep, given = halves(bott, bit, "proto", 0)
        bott = keep + swap(given, bit, "proto")
    bott, turned_far = together(bott, turn_rows(tokens_far))
    recip = lax.rsqrt(jnp.sum(bott * bott, axis=1, keepdims=True) + norm_eps)
    unit = bott * recip
    student_own = unit.astype(bf16)
    student_blocks = group_rows(student_own)
    run = functools.partial(
        softmax_pass,
        left=proto_student,
        value=proto_student,
        center=None,
        part=part,
        parts=4,
        tau=tau_student,
    )
    first = run(student_blocks[0][0])
    far_rows, *first = together(jnp.concatenate(student_blocks[1], 0), *first)
    second = run(far_rows)
    student_blocks[0][1], *second = together(student_blocks[0][1], *second)
    far_s = swap(second[1].astype(bf16), zlo)
    third = run(student_blocks[0][1])
    far_s, *third = together(far_s, *third)
    es, near_s, lse_s = gather_passes(first, second, third)
    mean_s, own_lse, lse_s, marks = merge(near_s, far_s, lse_s)

    weight_own = own_rows(weight[0][0])
    cross = own_lse / log2e - jnp.sum(student_own.astype(f32) * mean_t, axis=1) / tau_student
    loss = jnp.sum(weight_own * cross).reshape((1,))
    loss = loss + swap(loss, zhi)

    coef = loss_scale / tau_student
    dnorm = (coef * weight_own)[:, None] * (mean_s - mean_t)
    dbott_own = (recip * (dnorm - unit * jnp.sum(unit * dnorm, axis=1, keepdims=True))).astype(bf16)

    student_n = jnp.concatenate(
        [student_blocks[0][0], student_blocks[1][0], student_blocks[1][1], student_blocks[0][1]], 0
    )
    width = student_n.shape[1]
    share = width // row_size
    unit_index = jnp.arange(width, dtype=jnp.int32)
    source = ((unit_index // share) ^ row_index) * share + unit_index % share
    perm = (unit_index[:, None] == source[None, :]).astype(bf16)
    turned = lax.dot_general(
        perm, student_n, (((0,), (1,)), ((), ())), preferred_element_type=f32
    ).astype(bf16)

    def factors(passed, lse):
        out = []
        for (_, top), at in zip(passed, order_of):
            rows = jnp.concatenate([lse[z, c] for z, c in at])
            scale = jnp.concatenate([weight[z][c] for z, c in at])
            value = jnp.exp2(top - rows) * (coef * scale)
            out.append(jnp.broadcast_to(value[:, None], (value.shape[0], 128)))
        return out

    order_of = ([(0, 0)], [(1, 0), (1, 1)], [(0, 1)])
    scale_s = factors(es, lse_s)
    scale_t = factors(et, lse_t)
    count = es[0][0].shape[1]
    blocks = [(es[i][0], scale_s[i], et[i][0], scale_t[i]) for i in range(3)]

    def fold_y(value, *before):
        value = value.reshape((2, 2, 2, -1, value.shape[1]))
        sent = swap(after(value[:, :, 1], *before), ybit)
        return value[:, :, 0] + sent, sent

    def fold_h(value):
        return value[0] + swap(value[1], zhi)

    def fold(value):
        columns = value.shape[-1]
        value = value.reshape((2, 2, -1, columns))
        value = jnp.stack([value[:, 0], swap(value[:, 1], core)], 1)
        value = jnp.stack([value[0], swap(value[1], zlo)])
        return value.reshape((4, -1, columns))

    def spread(pieces):
        whole = jnp.concatenate(pieces, 2)
        return jnp.concatenate(
            [lax.dynamic_index_in_dim(whole, part ^ q, 0, False) for q in range(4)], 1
        ).astype(f32)

    pieces = 2 if (count // 2) % 128 == 0 else 1
    proto_pieces, sent = [], []
    for i in range(pieces):
        value = proto_pass(after(turned, marks[i]), blocks, i, pieces)
        value, got = fold_y(value)
        proto_pieces.append(value)
        sent.append(got)
    dbott = collect(dbott_own, "proto", proto_bits, 0)
    dbott, loss, proto_pieces[0] = together(dbott, loss, proto_pieces[0])
    dbott_far = swap(dbott, zlo)
    dbott = [
        jnp.concatenate([dbott, swap(dbott, core)], 0),
        jnp.concatenate([dbott_far, swap(dbott_far, core)], 0),
    ]
    proto_pieces[0] = fold(fold_h(proto_pieces[0]))

    hidden = [jnp.concatenate(pair, 1) for pair in hiddens]
    w_out_grad = (inner(hidden[0], dbott[0]) + inner(hidden[1], dbott[1])).astype(bf16)
    product = w_out_grad
    parts = 2
    back = [
        outer_last(dbott[z], w_out_part) * jnp.concatenate(slopes[z], 1).astype(f32)
        for z in (0, 1)
    ]
    back = [value.astype(bf16) for value in back]
    *back, product, proto_pieces[-1] = together(*back, product, proto_pieces[-1])
    proto_pieces = proto_pieces[:1] + [fold(fold_h(value)) for value in proto_pieces[1:]]
    keep, given = halves(product, ybit, "row", 0)
    w_out_grad = keep + swap(given, ybit)
    sums = []
    for i in range(parts):
        grad = grad_pass(turned_near, turned_far, *back, i, parts)
        grad, back[0] = together(grad, back[0])
        sums += [fold_y(half)[0] for half in jnp.split(grad, 2, axis=1)]
    keep, given = halves(w_out_grad, zhi, "row", 0)
    w_out_grad = keep + swap(given, zhi)
    w_out_grad = in_order(w_out_grad, swap(w_out_grad, zhi), zhi, "row", 0)
    w_out_grad, sums[0] = together(w_out_grad, sums[0])
    w_out_grad, sums[-1] = together(w_out_grad, sums[-1])
    w_out_grad = in_order(w_out_grad, swap(w_out_grad, ybit), ybit, "row", 0)
    w_out_grad = in_order(w_out_grad, swap(w_out_grad, zlo), zlo, "row", 0)
    sums = [fold_h(value) for value in sums]
    loss, sums[0] = together(loss, sums[0])
    loss = loss + swap(loss, ybit)
    for bit in proto_bits:
        loss = loss + swap(loss, bit, "proto")
    for bit in (core, zlo):
        loss = loss + swap(loss, bit)
    early = [fold(value) for value in sums[:-2]]
    loss, sums[-2], *early = together(loss, sums[-2], *early)
    loss = loss[0]
    w_in_pieces = early + [fold(value) for value in sums[-2:]]
    w_out_grad = w_out_grad.reshape((2, 1, quarter, -1))
    w_out_grad = in_order(w_out_grad, swap(w_out_grad, core), core, "row", 1)
    w_out_grad = w_out_grad.reshape((4 * quarter, -1))
    return (loss, spread(w_in_pieces), w_out_grad.astype(f32), spread(proto_pieces))


def solution(mesh):
    return jax.shard_map(
        on_device,
        mesh=mesh,
        in_specs=(
            P("row", None),
            P("row", "proto"),
            P("proto", None),
            P(("row", "proto"), None),
            P(None, "proto"),
            P(None, "proto"),
            P("proto"),
            P("row"),
        ),
        out_specs=(P(), P("row", "proto"), P("proto", None), P("row", "proto")),
        check_vma=False,
    )
```
